32 devices in a mesh: group: 2 (over x), ctx: 8 (over z, y), dp: 2 (over core).
Axes of the slice: x: 2, y: 2, z: 4, core: 2. Of those that a mesh axis runs over, the one named last changes fastest.
Arguments:
- tokens: bfloat16 [16384, 5120], P(('group', 'ctx')), parts along dimension 0, may hold values from -6 to 6
- cotangent: bfloat16 [16384, 1024], P(('group', 'ctx')), parts along dimension 0, may hold values from -0.1875 to 0.1875
- factor_a: float32 [512, 5120], P(('group', 'ctx')), parts along dimension 0, may hold values from -0.078125 to 0.078125
- factor_b: float32 [512, 1024], P(('group', 'ctx')), parts along dimension 0, may hold values from -0.1875 to 0.1875
- moment_a: float32 [512, 5120], P(('group', 'ctx', 'dp')), parts along dimension 0, may hold values from -3 to 3
- moment_b: float32 [512, 1024], P(('group', 'ctx', 'dp')), parts along dimension 0, may hold values from -3 to 3
- second_a: float32 [512, 5120], P(('group', 'ctx', 'dp')), parts along dimension 0, may hold values from 0.1 to 2
- second_b: float32 [512, 1024], P(('group', 'ctx', 'dp')), parts along dimension 0, may hold values from 0.1 to 2
- token_counts: int32 [16], P('group'), parts along dimension 0, may hold values from 1 to 2048, 8192 in all
- rank_blocks: int32 [16], P('group'), parts along dimension 0, may hold values from 1 to 16, 32 in all
Outputs:
- new_factor_a: float32 [512, 5120], P(('group', 'ctx')), parts along dimension 0
- new_factor_b: float32 [512, 1024], P(('group', 'ctx')), parts along dimension 0
- new_moment_a: float32 [512, 5120], P(('group', 'ctx', 'dp')), parts along dimension 0
- new_second_a: float32 [512, 5120], P(('group', 'ctx', 'dp')), parts along dimension 0
- new_moment_b: float32 [512, 1024], P(('group', 'ctx', 'dp')), parts along dimension 0
- new_second_b: float32 [512, 1024], P(('group', 'ctx', 'dp')), parts along dimension 0
The draws below stay inside these ranges and needn't reach their ends.
There are 2 independent parts, one for each index of `group`. The reference program is written for one: setup_inputs(seed, part) draws one part's arguments, and reference() takes and returns one part's arrays. A program takes and returns all parts, laid end to end along the dimension named above; each array names one. Nothing has to cross between parts.
Inputs may be any that keep to these rules, and one draw needn't show every extreme that they name: `token_counts`: the tenants' token segments fill the batch of 8192 tokens; the largest holds exactly 2048 tokens. The ranks 8 * rank_blocks sum to 256; the largest rank is exactly 128.
All inputs are finite; a program needn't handle non-finite values.
Results may differ from the reference program's by a relative error of at most 0.00088.
Values may be sent and summed in bfloat16 or wider, within the bound.
A program may use at most 64 MiB of HBM per device.

```python
import math
import jax
import jax.numpy as jnp
import numpy as np
from jax import lax

D = 5120
DOUT = 1024
TEN = 8
RTOT = 256
TOKENS = 8192


def shard_levels(key, extent, split, smallest, top_value):
    def one(dim, blocks):
        heights = jax.random.uniform(jax.random.fold_in(jax.random.fold_in(key, 6), dim), (blocks,), jnp.float32, smallest / len(split), top_value / len(split))
        return jnp.repeat(jnp.exp(heights), extent[dim] // blocks).reshape((-1,) + (1,) * (len(extent) - dim - 1))

    loudness = one(*split[0])
    for cut in split[1:]:
        loudness = loudness * one(*cut)
    return loudness


def split_up(amount, total, reach, lean):
    portions = [(1 << 20) // math.isqrt(standing ** lean) + 1 for standing in range(2, amount + 1)]
    spare, holding = total - reach - (amount - 1), [1] * (amount - 1)
    while spare > 0:
        candidates = [i for i in range(amount - 1) if holding[i] < reach]
        pool, remaining = sum([portions[i] for i in candidates]), spare
        for i in candidates:
            more = min(reach - holding[i], max(1, remaining * portions[i] // pool), spare)
            holding[i] = holding[i] + more
            spare = spare - more
    return np.array([reach] + holding)


def uneven_parts(rng, count, total, limit, skew):
    if count == 2:
        one = jax.random.randint(rng, (), max(1, total - limit), min(limit, total - 1) + 1)
        return jnp.stack([one, total - one])
    lengths = jnp.asarray(split_up(count, total, limit, skew), jnp.int32)
    couples = (count - 1) // 2
    source_of, sink = lengths[1:1 + 2 * couples:2], lengths[2:2 + 2 * couples:2]
    slack = jnp.minimum(source_of - 1, limit - sink)
    moved = jax.random.randint(jax.random.fold_in(rng, 1), (couples,), 0, 1 << 20) % (slack + 1)
    lengths = lengths.at[1:1 + 2 * couples:2].set(source_of - moved).at[2:2 + 2 * couples:2].set(sink + moved)
    return lengths[jax.random.permutation(jax.random.fold_in(rng, 2), count)]


def bell_draw(rng, extent, deviation, limit, split=(), held_as=jnp.bfloat16):
    drawn = deviation * jax.random.normal(rng, extent, jnp.float32)
    if split:
        drawn = drawn * shard_levels(rng, extent, split, -0.22, 0.18)
    return jnp.clip(drawn, -limit, limit).astype(held_as)


def setup_inputs(seed: int = 0, part: int = 0) -> dict:
    key_list = jax.random.split(jax.random.key(seed), 11)
    part_keys = jax.random.split(jax.random.fold_in(key_list[10], part), 11)
    tokens = bell_draw(part_keys[0], (TOKENS, D), 1.0, 6.0, ((0, 8),))
    cotangent = bell_draw(part_keys[1], (TOKENS, DOUT), ((TOKENS // TEN) ** -0.5), 0.1875, ((0, 8),))
    factor_a = bell_draw(part_keys[2], (RTOT, D), D ** -0.5, 0.078125, ((0, 8),), jnp.float32)
    factor_b = bell_draw(part_keys[3], (RTOT, DOUT), DOUT ** -0.5, 0.1875, ((0, 8),), jnp.float32)
    moment_a = bell_draw(part_keys[4], (RTOT, D), 0.5, 3.0, ((0, 16),), jnp.float32)
    moment_b = bell_draw(part_keys[5], (RTOT, DOUT), 0.5, 3.0, ((0, 16),), jnp.float32)
    second_a = jnp.clip(jnp.exp(math.log(2.0) - 2.9957323 * jax.random.uniform(part_keys[6], (RTOT, D), jnp.float32) ** shard_levels(part_keys[6], (RTOT, D), ((0, 16),), -0.2, 0.2)), 0.1, 2.0)
    second_b = jnp.clip(jnp.exp(math.log(2.0) - 2.9957323 * jax.random.uniform(part_keys[7], (RTOT, DOUT), jnp.float32) ** shard_levels(part_keys[7], (RTOT, DOUT), ((0, 16),), -0.2, 0.2)), 0.1, 2.0)
    token_counts = uneven_parts(part_keys[8], TEN, TOKENS, TOKENS // 4, 2).astype(jnp.int32)
    rank_blocks = uneven_parts(part_keys[9], TEN, RTOT // 8, 16, 2).astype(jnp.int32)
    return dict(tokens=tokens, cotangent=cotangent, factor_a=factor_a, factor_b=factor_b, moment_a=moment_a, moment_b=moment_b, second_a=second_a, second_b=second_b, token_counts=token_counts, rank_blocks=rank_blocks)


beta_one = 0.9
beta_two = 0.95
bias_one = 1.0 - 0.9 ** 10
bias_two = 1.0 - 0.95 ** 10
learn_rate = 0.01
decay_rate = 0.1
epsilon = 1e-08

def tenant_of(positions, ends):
    return lax.optimization_barrier(jnp.sum((positions[:, None] >= ends[None, :]).astype(jnp.int32), axis=1)).astype(jnp.int32)

def adamw(param, grad, moment, second):
    new_moment = beta_one * moment + (1.0 - beta_one) * grad
    new_second = beta_two * second + (1.0 - beta_two) * grad * grad
    update = new_moment / bias_one / (jnp.sqrt(new_second / bias_two) + epsilon)
    return (param - learn_rate * (update + decay_rate * param), new_moment, new_second)

def reference(tokens, cotangent, factor_a, factor_b, moment_a, moment_b, second_a, second_b, token_counts, rank_blocks):
    total_tokens = tokens.shape[0]
    total_rows = factor_a.shape[0]
    token_tenant = tenant_of(jnp.arange(total_tokens, dtype=jnp.int32), jnp.cumsum(token_counts).astype(jnp.int32))
    row_tenant = tenant_of(jnp.arange(total_rows, dtype=jnp.int32), jnp.cumsum(rank_blocks * 8).astype(jnp.int32))
    same_tenant = token_tenant[:, None] == row_tenant[None, :]
    low_a = factor_a.astype(jnp.bfloat16)
    low_b = factor_b.astype(jnp.bfloat16)
    scores_a = jnp.dot(tokens, low_a.T, preferred_element_type=jnp.float32)
    scores_b = jnp.dot(cotangent, low_b.T, preferred_element_type=jnp.float32)
    hidden = jnp.where(same_tenant, scores_a, 0.0).astype(jnp.bfloat16)
    back = jnp.where(same_tenant, scores_b, 0.0).astype(jnp.bfloat16)
    grad_a = jnp.dot(back.T, tokens, preferred_element_type=jnp.float32)
    grad_b = jnp.dot(hidden.T, cotangent, preferred_element_type=jnp.float32)
    new_a, new_moment_a, new_second_a = adamw(factor_a, grad_a, moment_a, second_a)
    new_b, new_moment_b, new_second_b = adamw(factor_b, grad_b, moment_b, second_b)
    return (new_a, new_b, new_moment_a, new_second_a, new_moment_b, new_second_b)
```

```python
import functools

import jax
import jax.numpy as jnp
from jax import lax
from jax.experimental import pallas as pl
from jax.experimental.pallas import tpu as pltpu
from jax.sharding import PartitionSpec as P

beta_one = 0.9
beta_two = 0.95
bias_one = 1.0 - 0.9**10
bias_two = 1.0 - 0.95**10
learn_rate = 0.01
decay_rate = 0.1
epsilon = 1e-08


def tenant_of(positions, ends):
    return jnp.sum((positions[:, None] >= ends[None, :]).astype(jnp.int32), axis=1)


def adamw(param, grad, moment, second):
    new_moment = beta_one * moment + (1.0 - beta_one) * grad
    new_second = beta_two * second + (1.0 - beta_two) * grad * grad
    update = new_moment / bias_one / (jnp.sqrt(new_second / bias_two) + epsilon)
    return (param - learn_rate * (update + decay_rate * param), new_moment, new_second)


def partial_grads(
    token_rows, grad_rows, low_a, low_b, positions, rank_rows, token_counts, rank_ends
):
    token_tenant = tenant_of(positions, jnp.cumsum(token_counts))
    row_tenant = tenant_of(rank_rows, rank_ends)
    same_tenant = token_tenant[:, None] == row_tenant[None, :]
    contract = (((1,), (1,)), ((), ()))
    scores_a = lax.dot_general(token_rows, low_a, contract, preferred_element_type=jnp.float32)
    scores_b = lax.dot_general(grad_rows, low_b, contract, preferred_element_type=jnp.float32)
    hidden = jnp.where(same_tenant, scores_a, 0.0).astype(jnp.bfloat16)
    back = jnp.where(same_tenant, scores_b, 0.0).astype(jnp.bfloat16)
    over_tokens = (((0,), (0,)), ((), ()))
    grad_a = lax.dot_general(back, token_rows, over_tokens, preferred_element_type=jnp.float32)
    grad_b = lax.dot_general(hidden, grad_rows, over_tokens, preferred_element_type=jnp.float32)
    return (grad_a, grad_b)


def local_plain(
    tokens,
    cotangent,
    factor_a,
    factor_b,
    moment_a,
    moment_b,
    second_a,
    second_b,
    token_counts,
    rank_blocks,
):
    tok_rows = tokens.shape[0]
    own_rows = moment_a.shape[0]
    context_index = lax.axis_index("ctx")
    replica_index = lax.axis_index("dp")
    rank_ends = jnp.cumsum(rank_blocks * 8)
    half_rows = tok_rows // 2
    token_rows = lax.dynamic_slice_in_dim(tokens, replica_index * half_rows, half_rows, 0)
    grad_rows = lax.dynamic_slice_in_dim(cotangent, replica_index * half_rows, half_rows, 0)
    positions = (
        context_index * tok_rows
        + replica_index * half_rows
        + jnp.arange(half_rows, dtype=jnp.int32)
    )
    all_a, all_b = (
        lax.all_gather(factor_a.astype(jnp.bfloat16), "ctx", axis=0, tiled=True),
        lax.all_gather(factor_b.astype(jnp.bfloat16), "ctx", axis=0, tiled=True),
    )
    rank_rows = jnp.arange(all_a.shape[0], dtype=jnp.int32)
    term_a, term_b = partial_grads(
        token_rows, grad_rows, all_a, all_b, positions, rank_rows, token_counts, rank_ends
    )
    grad_a, grad_b = (
        lax.psum_scatter(term_a, ("ctx", "dp"), scatter_dimension=0, tiled=True),
        lax.psum_scatter(term_b, ("ctx", "dp"), scatter_dimension=0, tiled=True),
    )
    owned_a = lax.dynamic_slice_in_dim(factor_a, replica_index * own_rows, own_rows, 0)
    owned_b = lax.dynamic_slice_in_dim(factor_b, replica_index * own_rows, own_rows, 0)
    step_a, new_moment_a, new_second_a = adamw(owned_a, grad_a, moment_a, second_a)
    step_b, new_moment_b, new_second_b = adamw(owned_b, grad_b, moment_b, second_b)
    new_a, new_b = (
        lax.all_gather(step_a, "dp", axis=0, tiled=True),
        lax.all_gather(step_b, "dp", axis=0, tiled=True),
    )
    return (new_a, new_b, new_moment_a, new_second_a, new_moment_b, new_second_b)


MESH = pl.DeviceIdType.MESH
HBM = pl.BlockSpec(memory_space=pl.ANY)
SMEM = pl.BlockSpec(memory_space=pltpu.SMEM)


def ring_kernel(
    n,
    chunks,
    tokens,
    cotangent,
    factor_a,
    factor_b,
    moment_a,
    moment_b,
    second_a,
    second_b,
    token_counts,
    rank_blocks,
    out_a,
    out_b,
    out_moment_a,
    out_second_a,
    out_moment_b,
    out_second_b,
    tok,
    cot,
    param,
    moment,
    second,
    low_a,
    low_b,
    back,
    hidden,
    scores,
    grads,
    whole_in,
    half_in,
    load_sem,
    store_sem,
    gather_send,
    gather_recv,
    reduce_send,
    reduce_recv,
    pair_send,
    pair_recv,
):
    hops = n // 2
    width_a = factor_a.shape[1]
    width_b = factor_b.shape[1]
    own = moment_a.shape[0]
    toks = tokens.shape[0]
    rows = n * own
    group = lax.axis_index("group")
    ctx = lax.axis_index("ctx")
    core = lax.axis_index("dp")
    column, odd = ctx // 2, ctx % 2
    place = column + odd * (n - 1 - 2 * column)

    def index_at(position):
        q = (position + 2 * n) % n
        return 2 * q + (q // hops) * (2 * n - 1 - 4 * q)

    def block(position):
        return pl.ds(pl.multiple_of(index_at(position) * own, own), own)

    signs = (1, -1)
    neighbours = [(group, index_at(place + s), core) for s in signs]
    partner = (group, ctx, 1 - core)
    my_half = pl.ds(pl.multiple_of(core * own, own), own)
    cols_a, cols_b = pl.ds(0, width_a), pl.ds(width_a, width_b)

    loads = [
        pltpu.make_async_copy(source, target, load_sem.at[i])
        for i, (source, target) in enumerate(
            (
                (factor_b.at[my_half], param.at[:, cols_b]),
                (factor_a.at[my_half], param.at[:, cols_a]),
                (cotangent, cot),
                (tokens, tok),
                (moment_a, moment.at[:, cols_a]),
                (moment_b, moment.at[:, cols_b]),
                (second_a, second.at[:, cols_a]),
                (second_b, second.at[:, cols_b]),
            )
        )
    ]
    for load in loads:
        load.start()
    barrier = pltpu.get_barrier_semaphore()
    for device in (*neighbours, partner):
        pl.semaphore_signal(barrier, inc=1, device_id=device, device_id_type=MESH)
    mine = block(place)
    loads[0].wait()
    low_b[mine, :] = param[:, width_a:].astype(jnp.bfloat16)
    loads[1].wait()
    low_a[mine, :] = param[:, :width_a].astype(jnp.bfloat16)
    pl.semaphore_wait(barrier, 3)

    sent = []

    def gather_copy(which, d, t):
        low, width = ((low_a, width_a), (low_b, width_b))[which]
        where = block(place - signs[d] * (t - 1))
        cols = pl.ds(d * (width // 2), width // 2) if t == hops else pl.ds(0, width)
        return pltpu.make_async_remote_copy(
            src_ref=low.at[where, cols],
            dst_ref=low.at[where, cols],
            send_sem=gather_send.at[which, d, t - 1],
            recv_sem=gather_recv.at[which, d, t - 1],
            device_id=neighbours[d],
            device_id_type=MESH,
        )

    def gather(which, t):
        for d in range(2):
            if t > 1:
                arrived[which, d].wait_recv()
            if t <= hops:
                copy = gather_copy(which, d, t)
                copy.start()
                arrived[which, d] = copy
                sent.append(copy)

    arrived = {}
    gather(1, 1)
    gather(0, 1)
    for t in range(2, hops + 1):
        gather(1, t)
    gather(0, 2)

    def tenant(position, counts, scale):
        total = jnp.zeros_like(position)
        end = 0
        for t in range(counts.shape[0]):
            end = end + counts[t] * scale
            total = total + (position >= end).astype(jnp.int32)
        return total

    row = lax.broadcasted_iota(jnp.int32, (rows, 1), 0)
    row = (row // own) * (2 * own) + core * own + row % own
    token = ctx * toks + lax.broadcasted_iota(jnp.int32, (1, toks), 1)
    same = tenant(row, rank_blocks, 8) == tenant(token, token_counts, 1)
    last = (((1,), (1,)), ((), ()))

    gather(1, hops + 1)
    loads[2].wait()
    scores_b = lax.dot_general(low_b[...], cot[...], last, preferred_element_type=jnp.float32)
    back[...] = jnp.where(same, scores_b, 0.0).astype(jnp.bfloat16)
    for t in range(3, hops):
        gather(0, t)

    reducing = {}

    def reduce_step(c, t):
        start, width = chunks[c]
        half = width // 2
        for d in range(2):
            if t > 1:
                reducing[c, d].wait_recv()
            if t > hops:
                continue
            where = block(place + signs[d] * (hops + 1 - t))
            if t == 1:
                source = grads.at[where, pl.ds(start + d * half, half)]
                target = half_in.at[d, :, pl.ds(start // 2, half)]
            else:
                if t == 2:
                    cols = pl.ds(start + d * half, half)
                    grads[where, cols] += half_in[d, :, start // 2 : start // 2 + half]
                else:
                    cols = pl.ds(start, width)
                    grads[where, cols] += whole_in[d, t - 3, :, start : start + width]
                source = grads.at[where, pl.ds(start, width)]
                target = whole_in.at[d, t - 2, :, pl.ds(start, width)]
            copy = pltpu.make_async_remote_copy(
                src_ref=source,
                dst_ref=target,
                send_sem=reduce_send.at[c, d, t - 1],
                recv_sem=reduce_recv.at[c, d, t - 1],
                device_id=neighbours[d],
                device_id_type=MESH,
            )
            copy.start()
            reducing[c, d] = copy
            sent.append(copy)

    loads[3].wait()
    last_c = len(chunks) - 1
    tile = 512

    def grad_tile(start):
        def body(i, carry):
            cols = pl.ds(pl.multiple_of(start + i * tile, tile), tile)
            grads[:, cols] = jnp.dot(
                back[...], tok[:, cols], preferred_element_type=jnp.float32
            )
            return carry

        return body

    for c in range(last_c):
        lax.fori_loop(0, chunks[c][1] // tile, grad_tile(chunks[c][0]), 0)
        reduce_step(c, 1)
        if c == 0:
            gather(0, hops)
    for c in range(last_c):
        reduce_step(c, 2)
    gather(0, hops + 1)

    depth = 1024
    scores[...] = jnp.zeros_like(scores)

    def score_tile(i, carry):
        cols = pl.ds(pl.multiple_of(i * depth, depth), depth)
        scores[...] += lax.dot_general(
            low_a[:, cols], tok[:, cols], last, preferred_element_type=jnp.float32
        )
        return carry

    lax.fori_loop(0, width_a // depth, score_tile, 0)
    hidden[...] = jnp.where(same, scores[...], 0.0).astype(jnp.bfloat16)
    grads[:, cols_b] = jnp.dot(hidden[...], cot[...], preferred_element_type=jnp.float32)
    reduce_step(last_c, 1)
    for t in range(3, hops + 1):
        for c in range(last_c):
            reduce_step(c, t)
        reduce_step(last_c, t - 1)

    for load in loads[4:]:
        load.wait()
    stores = []

    def finish(c):
        start, width = chunks[c]
        cols = pl.ds(start, width)
        reduce_step(c, hops + 1)
        grad = grads[mine, cols] + whole_in[0, hops - 2, :, start : start + width]
        grad = grad + whole_in[1, hops - 2, :, start : start + width]
        new = adamw(param[:, cols], grad, moment[:, cols], second[:, cols])
        param[:, cols], moment[:, cols], second[:, cols] = new
        if start < width_a:
            outs, at = (out_a, out_moment_a, out_second_a), pl.ds(start, width)
        else:
            outs, at = (out_b, out_moment_b, out_second_b), pl.ds(start - width_a, width)
        copy = pltpu.make_async_remote_copy(
            src_ref=param.at[:, cols],
            dst_ref=outs[0].at[my_half, at],
            send_sem=pair_send.at[c],
            recv_sem=pair_recv.at[c],
            device_id=partner,
            device_id_type=MESH,
        )
        copy.start()
        sent.append(copy)
        targets = (outs[0].at[my_half, at], outs[1].at[:, at], outs[2].at[:, at])
        for i, (source, target) in enumerate(zip((param, moment, second), targets)):
            store = pltpu.make_async_copy(source.at[:, cols], target, store_sem.at[c, i])
            store.start()
            stores.append(store)
        return copy

    pairs = []
    for c in range(last_c):
        pairs.append(finish(c))
        if c == 0:
            reduce_step(last_c, hops)
    pairs.append(finish(last_c))
    for pair in pairs:
        pair.wait_recv()
    for store in stores:
        store.wait()
    for copy in sent:
        copy.wait_send()


def local_ring(n, *args):
    tokens, cotangent, factor_a, factor_b, moment_a = args[:5]
    toks, width_a = tokens.shape
    width_b = cotangent.shape[1]
    own = moment_a.shape[0]
    width = width_a + width_b
    rows = n * own
    hops = n // 2
    half = width_a // 2
    chunks = ((0, half), (half, half), (width_a, width_b))
    f32, bf16 = jnp.float32, jnp.bfloat16
    count = len(chunks)
    dma = pltpu.SemaphoreType.DMA
    like = jax.ShapeDtypeStruct
    return pl.pallas_call(
        functools.partial(ring_kernel, n, chunks),
        out_shape=(
            like(factor_a.shape, f32),
            like(factor_b.shape, f32),
            like((own, width_a), f32),
            like((own, width_a), f32),
            like((own, width_b), f32),
            like((own, width_b), f32),
        ),
        in_specs=[HBM] * 8 + [SMEM] * 2,
        out_specs=(HBM,) * 6,
        scratch_shapes=[
            pltpu.VMEM((toks, width_a), bf16),
            pltpu.VMEM((toks, width_b), bf16),
            pltpu.VMEM((own, width), f32),
            pltpu.VMEM((own, width), f32),
            pltpu.VMEM((own, width), f32),
            pltpu.VMEM((rows, width_a), bf16),
            pltpu.VMEM((rows, width_b), bf16),
            pltpu.VMEM((rows, toks), bf16),
            pltpu.VMEM((rows, toks), bf16),
            pltpu.VMEM((rows, toks), f32),
            pltpu.VMEM((rows, width), f32),
            pltpu.VMEM((2, hops - 1, own, width), f32),
            pltpu.VMEM((2, own, width // 2), f32),
            dma((8,)),
            dma((count, 3)),
            dma((2, 2, hops)),
            dma((2, 2, hops)),
            dma((count, 2, hops)),
            dma((count, 2, hops)),
            dma((count,)),
            dma((count,)),
        ],
        compiler_params=pltpu.CompilerParams(
            collective_id=0, has_side_effects=True, vmem_limit_bytes=50 << 20
        ),
    )(*args)


def solution(mesh):
    n = mesh.shape["ctx"]
    if n >= 4 and n % 2 == 0 and 256 % (32 * n) == 0:
        local = functools.partial(local_ring, n)
    else:
        local = local_plain

    return jax.shard_map(
        local,
        mesh=mesh,
        in_specs=(
            P(("group", "ctx"), None),
            P(("group", "ctx"), None),
            P(("group", "ctx"), None),
            P(("group", "ctx"), None),
            P(("group", "ctx", "dp"), None),
            P(("group", "ctx", "dp"), None),
            P(("group", "ctx", "dp"), None),
            P(("group", "ctx", "dp"), None),
            P("group"),
            P("group"),
        ),
        out_specs=(
            P(("group", "ctx"), None),
            P(("group", "ctx"), None),
            P(("group", "ctx", "dp"), None),
            P(("group", "ctx", "dp"), None),
            P(("group", "ctx", "dp"), None),
            P(("group", "ctx", "dp"), None),
        ),
        check_vma=False,
    )
```

```python
import functools

import jax
import jax.numpy as jnp
from jax import lax
from jax.experimental import pallas as pl
from jax.experimental.pallas import tpu as pltpu
from jax.sharding import PartitionSpec as P

beta_one = 0.9
beta_two = 0.95
bias_one = 1.0 - 0.9**10
bias_two = 1.0 - 0.95**10
learn_rate = 0.01
decay_rate = 0.1
epsilon = 1e-08


def tenant_of(positions, ends):
    return jnp.sum((positions[:, None] >= ends[None, :]).astype(jnp.int32), axis=1)


def adamw(param, grad, moment, second):
    new_moment = beta_one * moment + (1.0 - beta_one) * grad
    new_second = beta_two * second + (1.0 - beta_two) * grad * grad
    update = new_moment / bias_one / (jnp.sqrt(new_second / bias_two) + epsilon)
    return (param - learn_rate * (update + decay_rate * param), new_moment, new_second)


def partial_grads(
    token_rows, grad_rows, low_a, low_b, positions, rank_rows, token_counts, rank_ends
):
    token_tenant = tenant_of(positions, jnp.cumsum(token_counts))
    row_tenant = tenant_of(rank_rows, rank_ends)
    same_tenant = token_tenant[:, None] == row_tenant[None, :]
    contract = (((1,), (1,)), ((), ()))
    scores_a = lax.dot_general(token_rows, low_a, contract, preferred_element_type=jnp.float32)
    scores_b = lax.dot_general(grad_rows, low_b, contract, preferred_element_type=jnp.float32)
    hidden = jnp.where(same_tenant, scores_a, 0.0).astype(jnp.bfloat16)
    back = jnp.where(same_tenant, scores_b, 0.0).astype(jnp.bfloat16)
    over_tokens = (((0,), (0,)), ((), ()))
    grad_a = lax.dot_general(back, token_rows, over_tokens, preferred_element_type=jnp.float32)
    grad_b = lax.dot_general(hidden, grad_rows, over_tokens, preferred_element_type=jnp.float32)
    return (grad_a, grad_b)


def local_plain(
    tokens,
    cotangent,
    factor_a,
    factor_b,
    moment_a,
    moment_b,
    second_a,
    second_b,
    token_counts,
    rank_blocks,
):
    tok_rows = tokens.shape[0]
    own_rows = moment_a.shape[0]
    context_index = lax.axis_index("ctx")
    replica_index = lax.axis_index("dp")
    rank_ends = jnp.cumsum(rank_blocks * 8)
    half_rows = tok_rows // 2
    token_rows = lax.dynamic_slice_in_dim(tokens, replica_index * half_rows, half_rows, 0)
    grad_rows = lax.dynamic_slice_in_dim(cotangent, replica_index * half_rows, half_rows, 0)
    positions = (
        context_index * tok_rows
        + replica_index * half_rows
        + jnp.arange(half_rows, dtype=jnp.int32)
    )
    all_a, all_b = (
        lax.all_gather(factor_a.astype(jnp.bfloat16), "ctx", axis=0, tiled=True),
        lax.all_gather(factor_b.astype(jnp.bfloat16), "ctx", axis=0, tiled=True),
    )
    rank_rows = jnp.arange(all_a.shape[0], dtype=jnp.int32)
    term_a, term_b = partial_grads(
        token_rows, grad_rows, all_a, all_b, positions, rank_rows, token_counts, rank_ends
    )
    grad_a, grad_b = (
        lax.psum_scatter(term_a, ("ctx", "dp"), scatter_dimension=0, tiled=True),
        lax.psum_scatter(term_b, ("ctx", "dp"), scatter_dimension=0, tiled=True),
    )
    owned_a = lax.dynamic_slice_in_dim(factor_a, replica_index * own_rows, own_rows, 0)
    owned_b = lax.dynamic_slice_in_dim(factor_b, replica_index * own_rows, own_rows, 0)
    step_a, new_moment_a, new_second_a = adamw(owned_a, grad_a, moment_a, second_a)
    step_b, new_moment_b, new_second_b = adamw(owned_b, grad_b, moment_b, second_b)
    new_a, new_b = (
        lax.all_gather(step_a, "dp", axis=0, tiled=True),
        lax.all_gather(step_b, "dp", axis=0, tiled=True),
    )
    return (new_a, new_b, new_moment_a, new_second_a, new_moment_b, new_second_b)


MESH = pl.DeviceIdType.MESH
ANY = pl.BlockSpec(memory_space=pl.ANY)
HBM = pl.BlockSpec(memory_space=pltpu.HBM)


def ring_kernel(
    n,
    chunks,
    tokens,
    cotangent,
    factor_a,
    factor_b,
    moment_a,
    moment_b,
    second_a,
    second_b,
    token_counts,
    rank_blocks,
    out_a,
    out_b,
    out_moment_a,
    out_second_a,
    out_moment_b,
    out_second_b,
    tok,
    cot,
    param,
    moment,
    second,
    low_a,
    low_b,
    back,
    hidden,
    scores,
    grads,
    whole_in,
    half_in,
    counts,
    blocks,
    load_sem,
    store_sem,
    gather_send,
    gather_recv,
    reduce_send,
    reduce_recv,
    pair_send,
    pair_recv,
):
    hops = n // 2
    width_a = factor_a.shape[1]
    width_b = factor_b.shape[1]
    own = moment_a.shape[0]
    toks = tokens.shape[0]
    rows = n * own
    group = lax.axis_index("group")
    ctx = lax.axis_index("ctx")
    core = lax.axis_index("dp")
    column, odd = ctx // 2, ctx % 2
    place = column + odd * (n - 1 - 2 * column)

    def index_at(position):
        q = (position + 2 * n) % n
        return 2 * q + (q // hops) * (2 * n - 1 - 4 * q)

    def block(position):
        return pl.ds(pl.multiple_of(index_at(position) * own, own), own)

    signs = (1, -1)
    neighbours = [(group, index_at(place + s), core) for s in signs]
    partner = (group, ctx, 1 - core)
    my_half = pl.ds(pl.multiple_of(core * own, own), own)
    cols_a, cols_b = pl.ds(0, width_a), pl.ds(width_a, width_b)

    loads = [
        pltpu.make_async_copy(source, target, load_sem.at[i])
        for i, (source, target) in enumerate(
            (
                (factor_b.at[my_half], param.at[:, cols_b]),
                (factor_a.at[my_half], param.at[:, cols_a]),
                (cotangent, cot),
                (tokens, tok),
                (moment_a, moment.at[:, cols_a]),
                (moment_b, moment.at[:, cols_b]),
                (second_a, second.at[:, cols_a]),
                (second_b, second.at[:, cols_b]),
                (token_counts, counts),
                (rank_blocks, blocks),
            )
        )
    ]
    for load in loads:
        load.start()
    barrier = pltpu.get_barrier_semaphore()
    for device in (*neighbours, partner):
        pl.semaphore_signal(barrier, inc=1, device_id=device, device_id_type=MESH)
    mine = block(place)
    loads[0].wait()
    low_b[mine, :] = param[:, width_a:].astype(jnp.bfloat16)
    loads[1].wait()
    low_a[mine, :] = param[:, :width_a].astype(jnp.bfloat16)
    pl.semaphore_wait(barrier, 3)

    sent = []

    quarter = width_a // 2
    pieces = ((low_a, 0, quarter), (low_a, quarter, quarter), (low_b, 0, width_b))
    gathering = {}

    def gather(which, t):
        low, start, width = pieces[which]
        half = width // 2
        for d in range(2):
            if t > 1:
                gathering[which, d].wait_recv()
            if t > hops:
                continue
            where = block(place - signs[d] * (t - 1))
            cols = pl.ds(start + d * half, half) if t == hops else pl.ds(start, width)
            copy = pltpu.make_async_remote_copy(
                src_ref=low.at[where, cols],
                dst_ref=low.at[where, cols],
                send_sem=gather_send.at[which, d, t - 1],
                recv_sem=gather_recv.at[which, d, t - 1],
                device_id=neighbours[d],
                device_id_type=MESH,
            )
            copy.start()
            gathering[which, d] = copy
            sent.append(copy)

    gather(2, 1)
    gather(0, 1)
    gather(2, 2)
    gather(1, 1)
    for t in range(3, hops + 1):
        gather(2, t)
        gather(0, t - 1)
    for t in range(2, hops - 1):
        gather(1, t)

    def tenant(position, counts, scale):
        total = jnp.zeros_like(position)
        end = 0
        for t in range(counts.shape[0]):
            end = end + counts[t] * scale
            total = total + (position >= end).astype(jnp.int32)
        return total

    row = lax.broadcasted_iota(jnp.int32, (rows, 1), 0)
    row = (row // own) * (2 * own) + core * own + row % own
    token = ctx * toks + lax.broadcasted_iota(jnp.int32, (1, toks), 1)
    loads[8].wait()
    loads[9].wait()
    same = tenant(row, blocks, 8) == tenant(token, counts, 1)
    last = (((1,), (1,)), ((), ()))

    gather(2, hops + 1)
    loads[2].wait()
    scores_b = lax.dot_general(low_b[...], cot[...], last, preferred_element_type=jnp.float32)
    back[...] = jnp.where(same, scores_b, 0.0).astype(jnp.bfloat16)
    gather(1, hops - 1)

    reducing = {}

    def reduce_step(c, t):
        start, width = chunks[c]
        half = width // 2
        for d in range(2):
            if t > 1:
                reducing[c, d].wait_recv()
            if t > hops:
                continue
            where = block(place + signs[d] * (hops + 1 - t))
            if t == 1:
                source = grads.at[where, pl.ds(start + d * half, half)]
                target = half_in.at[d, :, pl.ds(start // 2, half)]
            else:
                if t == 2:
                    cols = pl.ds(start + d * half, half)
                    grads[where, cols] += half_in[d, :, start // 2 : start // 2 + half]
                else:
                    cols = pl.ds(start, width)
                    grads[where, cols] += whole_in[d, t - 3, :, start : start + width]
                source = grads.at[where, pl.ds(start, width)]
                target = whole_in.at[d, t - 2, :, pl.ds(start, width)]
            copy = pltpu.make_async_remote_copy(
                src_ref=source,
                dst_ref=target,
                send_sem=reduce_send.at[c, d, t - 1],
                recv_sem=reduce_recv.at[c, d, t - 1],
                device_id=neighbours[d],
                device_id_type=MESH,
            )
            copy.start()
            reducing[c, d] = copy
            sent.append(copy)

    loads[3].wait()
    last_c = len(chunks) - 1
    for c in range(last_c):
        start, width = chunks[c]
        grads[:, start : start + width] = jnp.dot(
            back[...], tok[:, start : start + width], preferred_element_type=jnp.float32
        )
        reduce_step(c, 1)
        if c < 2:
            gather(c, hops)
    for c in range(last_c):
        reduce_step(c, 2)
    gather(0, hops + 1)
    gather(1, hops + 1)

    depth = 1024
    scores[...] = jnp.zeros_like(scores)

    def score_tile(i, carry):
        cols = pl.ds(pl.multiple_of(i * depth, depth), depth)
        scores[...] += lax.dot_general(
            low_a[:, cols], tok[:, cols], last, preferred_element_type=jnp.float32
        )
        return carry

    lax.fori_loop(0, width_a // depth, score_tile, 0)
    hidden[...] = jnp.where(same, scores[...], 0.0).astype(jnp.bfloat16)
    grads[:, cols_b] = jnp.dot(hidden[...], cot[...], preferred_element_type=jnp.float32)
    reduce_step(last_c, 1)
    middle = last_c // 2
    reduce_step(0, 3)
    reduce_step(last_c, 2)
    for t in range(3, hops + 1):
        for c in range(last_c):
            if (c, t) != (0, 3):
                reduce_step(c, t)
            if c == middle:
                reduce_step(last_c, t)

    for load in loads[4:8]:
        load.wait()
    stores = []

    def finish(c):
        start, width = chunks[c]
        cols = pl.ds(start, width)
        reduce_step(c, hops + 1)
        grad = grads[mine, cols] + whole_in[0, hops - 2, :, start : start + width]
        grad = grad + whole_in[1, hops - 2, :, start : start + width]
        new = adamw(param[:, cols], grad, moment[:, cols], second[:, cols])
        param[:, cols], moment[:, cols], second[:, cols] = new
        if start < width_a:
            outs, at = (out_a, out_moment_a, out_second_a), pl.ds(start, width)
        else:
            outs, at = (out_b, out_moment_b, out_second_b), pl.ds(start - width_a, width)
        copy = pltpu.make_async_remote_copy(
            src_ref=param.at[:, cols],
            dst_ref=outs[0].at[my_half, at],
            send_sem=pair_send.at[c],
            recv_sem=pair_recv.at[c],
            device_id=partner,
            device_id_type=MESH,
        )
        copy.start()
        sent.append(copy)
        targets = (outs[0].at[my_half, at], outs[1].at[:, at], outs[2].at[:, at])
        for i, (source, target) in enumerate(zip((param, moment, second), targets)):
            store = pltpu.make_async_copy(source.at[:, cols], target, store_sem.at[c, i])
            store.start()
            stores.append(store)
        return copy

    pairs = [finish(c) for c in (0, last_c, *range(1, last_c))]
    for pair in pairs:
        pair.wait_recv()
    for store in stores:
        store.wait()
    for copy in sent:
        copy.wait_send()


def hand_out(*refs):
    copies = [
        pltpu.make_async_copy(refs[i], refs[6 + i], refs[12].at[i]) for i in range(6)
    ]
    for copy in copies:
        copy.start()
    for copy in copies:
        copy.wait()


def local_ring(n, *args):
    tokens, cotangent, factor_a, factor_b, moment_a = args[:5]
    toks, width_a = tokens.shape
    width_b = cotangent.shape[1]
    own = moment_a.shape[0]
    width = width_a + width_b
    rows = n * own
    hops = n // 2
    part = width_a // 4
    chunks = (*((i * part, part) for i in range(4)), (width_a, width_b))
    f32, bf16 = jnp.float32, jnp.bfloat16
    count = len(chunks)
    dma = pltpu.SemaphoreType.DMA
    like = jax.ShapeDtypeStruct
    results = pl.pallas_call(
        functools.partial(ring_kernel, n, chunks),
        out_shape=(
            like(factor_a.shape, f32),
            like(factor_b.shape, f32),
            like((own, width_a), f32),
            like((own, width_a), f32),
            like((own, width_b), f32),
            like((own, width_b), f32),
        ),
        in_specs=[HBM] * 10,
        out_specs=(ANY,) * 6,
        scratch_shapes=[
            pltpu.VMEM((toks, width_a), bf16),
            pltpu.VMEM((toks, width_b), bf16),
            pltpu.VMEM((own, width), f32),
            pltpu.VMEM((own, width), f32),
            pltpu.VMEM((own, width), f32),
            pltpu.VMEM((rows, width_a), bf16),
            pltpu.VMEM((rows, width_b), bf16),
            pltpu.VMEM((rows, toks), bf16),
            pltpu.VMEM((rows, toks), bf16),
            pltpu.VMEM((rows, toks), f32),
            pltpu.VMEM((rows, width), f32),
            pltpu.VMEM((2, hops - 1, own, width), f32),
            pltpu.VMEM((2, own, width // 2), f32),
            pltpu.SMEM(args[8].shape, jnp.int32),
            pltpu.SMEM(args[9].shape, jnp.int32),
            dma((10,)),
            dma((count, 3)),
            dma((3, 2, hops)),
            dma((3, 2, hops)),
            dma((count, 2, hops)),
            dma((count, 2, hops)),
            dma((count,)),
            dma((count,)),
        ],
        compiler_params=pltpu.CompilerParams(
            collective_id=0, has_side_effects=True, vmem_limit_bytes=63 << 20
        ),
    )(*args)
    return pl.pallas_call(
        hand_out,
        out_shape=tuple(like(r.shape, r.dtype) for r in results),
        in_specs=[ANY] * 6,
        out_specs=(HBM,) * 6,
        scratch_shapes=[dma((6,))],
    )(*results)


def solution(mesh):
    n = mesh.shape["ctx"]
    if n >= 4 and n % 2 == 0 and 256 % (32 * n) == 0:
        local = functools.partial(local_ring, n)
    else:
        local = local_plain

    return jax.shard_map(
        local,
        mesh=mesh,
        in_specs=(
            P(("group", "ctx"), None),
            P(("group", "ctx"), None),
            P(("group", "ctx"), None),
            P(("group", "ctx"), None),
            P(("group", "ctx", "dp"), None),
            P(("group", "ctx", "dp"), None),
            P(("group", "ctx", "dp"), None),
            P(("group", "ctx", "dp"), None),
            P("group"),
            P("group"),
        ),
        out_specs=(
            P(("group", "ctx"), None),
            P(("group", "ctx"), None),
            P(("group", "ctx", "dp"), None),
            P(("group", "ctx", "dp"), None),
            P(("group", "ctx", "dp"), None),
            P(("group", "ctx", "dp"), None),
        ),
        check_vma=False,
    )
```

```python
import functools

import jax
import jax.numpy as jnp
from jax import lax
from jax.experimental import pallas as pl
from jax.experimental.pallas import tpu as pltpu
from jax.sharding import PartitionSpec as P

beta_one = 0.9
beta_two = 0.95
bias_one = 1.0 - 0.9**10
bias_two = 1.0 - 0.95**10
learn_rate = 0.01
decay_rate = 0.1
epsilon = 1e-08


def tenant_of(positions, ends):
    return jnp.sum((positions[:, None] >= ends[None, :]).astype(jnp.int32), axis=1)


def adamw(param, grad, moment, second):
    new_moment = beta_one * moment + (1.0 - beta_one) * grad
    new_second = beta_two * second + (1.0 - beta_two) * grad * grad
    update = new_moment / bias_one / (jnp.sqrt(new_second / bias_two) + epsilon)
    return (param - learn_rate * (update + decay_rate * param), new_moment, new_second)


def partial_grads(
    token_rows, grad_rows, low_a, low_b, positions, rank_rows, token_counts, rank_ends
):
    token_tenant = tenant_of(positions, jnp.cumsum(token_counts))
    row_tenant = tenant_of(rank_rows, rank_ends)
    same_tenant = token_tenant[:, None] == row_tenant[None, :]
    contract = (((1,), (1,)), ((), ()))
    scores_a = lax.dot_general(token_rows, low_a, contract, preferred_element_type=jnp.float32)
    scores_b = lax.dot_general(grad_rows, low_b, contract, preferred_element_type=jnp.float32)
    hidden = jnp.where(same_tenant, scores_a, 0.0).astype(jnp.bfloat16)
    back = jnp.where(same_tenant, scores_b, 0.0).astype(jnp.bfloat16)
    over_tokens = (((0,), (0,)), ((), ()))
    grad_a = lax.dot_general(back, token_rows, over_tokens, preferred_element_type=jnp.float32)
    grad_b = lax.dot_general(hidden, grad_rows, over_tokens, preferred_element_type=jnp.float32)
    return (grad_a, grad_b)


def local_plain(
    tokens,
    cotangent,
    factor_a,
    factor_b,
    moment_a,
    moment_b,
    second_a,
    second_b,
    token_counts,
    rank_blocks,
):
    tok_rows = tokens.shape[0]
    own_rows = moment_a.shape[0]
    context_index = lax.axis_index("ctx")
    replica_index = lax.axis_index("dp")
    rank_ends = jnp.cumsum(rank_blocks * 8)
    half_rows = tok_rows // 2
    token_rows = lax.dynamic_slice_in_dim(tokens, replica_index * half_rows, half_rows, 0)
    grad_rows = lax.dynamic_slice_in_dim(cotangent, replica_index * half_rows, half_rows, 0)
    positions = (
        context_index * tok_rows
        + replica_index * half_rows
        + jnp.arange(half_rows, dtype=jnp.int32)
    )
    all_a, all_b = (
        lax.all_gather(factor_a.astype(jnp.bfloat16), "ctx", axis=0, tiled=True),
        lax.all_gather(factor_b.astype(jnp.bfloat16), "ctx", axis=0, tiled=True),
    )
    rank_rows = jnp.arange(all_a.shape[0], dtype=jnp.int32)
    term_a, term_b = partial_grads(
        token_rows, grad_rows, all_a, all_b, positions, rank_rows, token_counts, rank_ends
    )
    grad_a, grad_b = (
        lax.psum_scatter(term_a, ("ctx", "dp"), scatter_dimension=0, tiled=True),
        lax.psum_scatter(term_b, ("ctx", "dp"), scatter_dimension=0, tiled=True),
    )
    owned_a = lax.dynamic_slice_in_dim(factor_a, replica_index * own_rows, own_rows, 0)
    owned_b = lax.dynamic_slice_in_dim(factor_b, replica_index * own_rows, own_rows, 0)
    step_a, new_moment_a, new_second_a = adamw(owned_a, grad_a, moment_a, second_a)
    step_b, new_moment_b, new_second_b = adamw(owned_b, grad_b, moment_b, second_b)
    new_a, new_b = (
        lax.all_gather(step_a, "dp", axis=0, tiled=True),
        lax.all_gather(step_b, "dp", axis=0, tiled=True),
    )
    return (new_a, new_b, new_moment_a, new_second_a, new_moment_b, new_second_b)


MESH = pl.DeviceIdType.MESH
ANY = pl.BlockSpec(memory_space=pl.ANY)
VMEM = pl.BlockSpec(memory_space=pltpu.VMEM)
HBM = pl.BlockSpec(memory_space=pltpu.HBM)


def ring_kernel(
    n,
    chunks,
    tokens,
    cotangent,
    factor_a,
    factor_b,
    moment_a,
    moment_b,
    second_a,
    second_b,
    token_counts,
    rank_blocks,
    out_a,
    out_b,
    out_moment_a,
    out_second_a,
    out_moment_b,
    out_second_b,
    tok,
    cot,
    param,
    moment,
    second,
    low_a,
    low_b,
    back,
    hidden,
    scores,
    grads,
    whole_in,
    half_in,
    counts,
    blocks,
    load_sem,
    gather_send,
    gather_recv,
    reduce_send,
    reduce_recv,
    pair_send,
    pair_recv,
):
    hops = n // 2
    width_a = factor_a.shape[1]
    width_b = factor_b.shape[1]
    own = moment_a.shape[0]
    toks = tokens.shape[0]
    rows = n * own
    group = lax.axis_index("group")
    ctx = lax.axis_index("ctx")
    core = lax.axis_index("dp")
    column, odd = ctx // 2, ctx % 2
    place = column + odd * (n - 1 - 2 * column)

    def index_at(position):
        q = (position + 2 * n) % n
        return 2 * q + (q // hops) * (2 * n - 1 - 4 * q)

    def block(position):
        return pl.ds(pl.multiple_of(index_at(position) * own, own), own)

    signs = (1, -1)
    neighbours = [(group, index_at(place + s), core) for s in signs]
    partner = (group, ctx, 1 - core)
    my_half = pl.ds(pl.multiple_of(core * own, own), own)
    cols_a, cols_b = pl.ds(0, width_a), pl.ds(width_a, width_b)

    loads = [
        pltpu.make_async_copy(source, target, load_sem.at[i])
        for i, (source, target) in enumerate(
            (
                (factor_b.at[my_half], param.at[:, cols_b]),
                (factor_a.at[my_half], param.at[:, cols_a]),
                (cotangent, cot),
                (tokens, tok),
                (moment_a, moment.at[:, cols_a]),
                (moment_b, moment.at[:, cols_b]),
                (second_a, second.at[:, cols_a]),
                (second_b, second.at[:, cols_b]),
                (token_counts, counts),
                (rank_blocks, blocks),
            )
        )
    ]
    for load in loads:
        load.start()
    barrier = pltpu.get_barrier_semaphore()
    for device in (*neighbours, partner):
        pl.semaphore_signal(barrier, inc=1, device_id=device, device_id_type=MESH)
    mine = block(place)
    loads[0].wait()
    low_b[mine, :] = param[:, width_a:].astype(jnp.bfloat16)
    loads[1].wait()
    low_a[mine, :] = param[:, :width_a].astype(jnp.bfloat16)
    pl.semaphore_wait(barrier, 3)

    sent = []

    quarter = width_a // 2
    pieces = ((low_a, 0, quarter), (low_a, quarter, quarter), (low_b, 0, width_b))
    gathering = {}

    def gather(which, t):
        low, start, width = pieces[which]
        half = width // 2
        for d in range(2):
            if t > 1:
                gathering[which, d].wait_recv()
            if t > hops:
                continue
            where = block(place - signs[d] * (t - 1))
            cols = pl.ds(start + d * half, half) if t == hops else pl.ds(start, width)
            copy = pltpu.make_async_remote_copy(
                src_ref=low.at[where, cols],
                dst_ref=low.at[where, cols],
                send_sem=gather_send.at[which, d, t - 1],
                recv_sem=gather_recv.at[which, d, t - 1],
                device_id=neighbours[d],
                device_id_type=MESH,
            )
            copy.start()
            gathering[which, d] = copy
            sent.append(copy)

    gather(2, 1)
    gather(0, 1)
    gather(2, 2)
    gather(1, 1)
    for t in range(3, hops + 1):
        gather(2, t)
        gather(0, t - 1)
    for t in range(2, hops - 1):
        gather(1, t)

    def tenant(position, counts, scale):
        total = jnp.zeros_like(position)
        end = 0
        for t in range(counts.shape[0]):
            end = end + counts[t] * scale
            total = total + (position >= end).astype(jnp.int32)
        return total

    row = lax.broadcasted_iota(jnp.int32, (rows, 1), 0)
    row = (row // own) * (2 * own) + core * own + row % own
    token = ctx * toks + lax.broadcasted_iota(jnp.int32, (1, toks), 1)
    loads[8].wait()
    loads[9].wait()
    same = tenant(row, blocks, 8) == tenant(token, counts, 1)
    last = (((1,), (1,)), ((), ()))

    gather(2, hops + 1)
    loads[2].wait()
    scores_b = lax.dot_general(low_b[...], cot[...], last, preferred_element_type=jnp.float32)
    back[...] = jnp.where(same, scores_b, 0.0).astype(jnp.bfloat16)
    gather(1, hops - 1)

    reducing = {}

    def reduce_step(c, t):
        start, width = chunks[c]
        half = width // 2
        for d in range(2):
            if t > 1:
                reducing[c, d].wait_recv()
            if t > hops:
                continue
            where = block(place + signs[d] * (hops + 1 - t))
            if t == 1:
                source = grads.at[where, pl.ds(start + d * half, half)]
                target = half_in.at[d, :, pl.ds(start // 2, half)]
            else:
                if t == 2:
                    cols = pl.ds(start + d * half, half)
                    grads[where, cols] += half_in[d, :, start // 2 : start // 2 + half]
                else:
                    cols = pl.ds(start, width)
                    grads[where, cols] += whole_in[d, t - 3, :, start : start + width]
                source = grads.at[where, pl.ds(start, width)]
                target = whole_in.at[d, t - 2, :, pl.ds(start, width)]
            copy = pltpu.make_async_remote_copy(
                src_ref=source,
                dst_ref=target,
                send_sem=reduce_send.at[c, d, t - 1],
                recv_sem=reduce_recv.at[c, d, t - 1],
                device_id=neighbours[d],
                device_id_type=MESH,
            )
            copy.start()
            reducing[c, d] = copy
            sent.append(copy)

    loads[3].wait()
    last_c = len(chunks) - 1
    for c in range(last_c):
        start, width = chunks[c]
        grads[:, start : start + width] = jnp.dot(
            back[...], tok[:, start : start + width], preferred_element_type=jnp.float32
        )
        reduce_step(c, 1)
        if c < 2:
            gather(c, hops)
    for c in range(last_c):
        reduce_step(c, 2)
    gather(0, hops + 1)
    gather(1, hops + 1)

    depth = 1024
    scores[...] = jnp.zeros_like(scores)

    def score_tile(i, carry):
        cols = pl.ds(pl.multiple_of(i * depth, depth), depth)
        scores[...] += lax.dot_general(
            low_a[:, cols], tok[:, cols], last, preferred_element_type=jnp.float32
        )
        return carry

    lax.fori_loop(0, width_a // depth, score_tile, 0)
    hidden[...] = jnp.where(same, scores[...], 0.0).astype(jnp.bfloat16)
    grads[:, cols_b] = jnp.dot(hidden[...], cot[...], preferred_element_type=jnp.float32)
    reduce_step(last_c, 1)
    middle = last_c // 2
    reduce_step(0, 3)
    reduce_step(last_c, 2)
    for t in range(3, hops + 1):
        for c in range(last_c):
            if (c, t) != (0, 3):
                reduce_step(c, t)
            if c == middle:
                reduce_step(last_c, t)

    for load in loads[4:8]:
        load.wait()

    def finish(c):
        start, width = chunks[c]
        cols = pl.ds(start, width)
        reduce_step(c, hops + 1)
        grad = grads[mine, cols] + whole_in[0, hops - 2, :, start : start + width]
        grad = grad + whole_in[1, hops - 2, :, start : start + width]
        new = adamw(param[:, cols], grad, moment[:, cols], second[:, cols])
        if start < width_a:
            outs, at = (out_a, out_moment_a, out_second_a), pl.ds(start, width)
        else:
            outs, at = (out_b, out_moment_b, out_second_b), pl.ds(start - width_a, width)
        outs[0][my_half, at], outs[1][:, at], outs[2][:, at] = new
        copy = pltpu.make_async_remote_copy(
            src_ref=outs[0].at[my_half, at],
            dst_ref=outs[0].at[my_half, at],
            send_sem=pair_send.at[c],
            recv_sem=pair_recv.at[c],
            device_id=partner,
            device_id_type=MESH,
        )
        copy.start()
        sent.append(copy)
        return copy

    pairs = [finish(c) for c in (0, last_c, *range(1, last_c))]
    for pair in pairs:
        pair.wait_recv()
    for copy in sent:
        copy.wait_send()


def hand_out(*refs):
    copies = [
        pltpu.make_async_copy(refs[i], refs[6 + i], refs[12].at[i]) for i in range(6)
    ]
    for copy in copies:
        copy.start()
    for copy in copies:
        copy.wait()


def local_ring(n, *args):
    tokens, cotangent, factor_a, factor_b, moment_a = args[:5]
    toks, width_a = tokens.shape
    width_b = cotangent.shape[1]
    own = moment_a.shape[0]
    width = width_a + width_b
    rows = n * own
    hops = n // 2
    part = width_a // 4
    chunks = (*((i * part, part) for i in range(4)), (width_a, width_b))
    f32, bf16 = jnp.float32, jnp.bfloat16
    count = len(chunks)
    dma = pltpu.SemaphoreType.DMA
    like = jax.ShapeDtypeStruct
    results = pl.pallas_call(
        functools.partial(ring_kernel, n, chunks),
        out_shape=(
            pltpu.VMEM(factor_a.shape, f32),
            pltpu.VMEM(factor_b.shape, f32),
            pltpu.VMEM((own, width_a), f32),
            pltpu.VMEM((own, width_a), f32),
            pltpu.VMEM((own, width_b), f32),
            pltpu.VMEM((own, width_b), f32),
        ),
        in_specs=[HBM] * 10,
        out_specs=(VMEM,) * 6,
        scratch_shapes=[
            pltpu.VMEM((toks, width_a), bf16),
            pltpu.VMEM((toks, width_b), bf16),
            pltpu.VMEM((own, width), f32),
            pltpu.VMEM((own, width), f32),
            pltpu.VMEM((own, width), f32),
            pltpu.VMEM((rows, width_a), bf16),
            pltpu.VMEM((rows, width_b), bf16),
            pltpu.VMEM((rows, toks), bf16),
            pltpu.VMEM((rows, toks), bf16),
            pltpu.VMEM((rows, toks), f32),
            pltpu.VMEM((rows, width), f32),
            pltpu.VMEM((2, hops - 1, own, width), f32),
            pltpu.VMEM((2, own, width // 2), f32),
            pltpu.SMEM(args[8].shape, jnp.int32),
            pltpu.SMEM(args[9].shape, jnp.int32),
            dma((10,)),
            dma((3, 2, hops)),
            dma((3, 2, hops)),
            dma((count, 2, hops)),
            dma((count, 2, hops)),
            dma((count,)),
            dma((count,)),
        ],
        compiler_params=pltpu.CompilerParams(
            collective_id=0, has_side_effects=True, vmem_limit_bytes=50 << 20
        ),
    )(*(pltpu.with_memory_space_constraint(arg, pltpu.HBM) for arg in args))
    return pl.pallas_call(
        hand_out,
        out_shape=tuple(like(r.shape, r.dtype) for r in results),
        in_specs=[VMEM] * 6,
        out_specs=(HBM,) * 6,
        scratch_shapes=[dma((6,))],
    )(*results)


def solution(mesh):
    n = mesh.shape["ctx"]
    if n >= 4 and n % 2 == 0 and 256 % (32 * n) == 0:
        local = functools.partial(local_ring, n)
    else:
        local = local_plain

    return jax.shard_map(
        local,
        mesh=mesh,
        in_specs=(
            P(("group", "ctx"), None),
            P(("group", "ctx"), None),
            P(("group", "ctx"), None),
            P(("group", "ctx"), None),
            P(("group", "ctx", "dp"), None),
            P(("group", "ctx", "dp"), None),
            P(("group", "ctx", "dp"), None),
            P(("group", "ctx", "dp"), None),
            P("group"),
            P("group"),
        ),
        out_specs=(
            P(("group", "ctx"), None),
            P(("group", "ctx"), None),
            P(("group", "ctx", "dp"), None),
            P(("group", "ctx", "dp"), None),
            P(("group", "ctx", "dp"), None),
            P(("group", "ctx", "dp"), None),
        ),
        check_vma=False,
    )
```

```python
import functools

import jax
import jax.numpy as jnp
from jax import lax
from jax.experimental import pallas as pl
from jax.experimental.pallas import tpu as pltpu
from jax.sharding import PartitionSpec as P

beta_one = 0.9
beta_two = 0.95
bias_one = 1.0 - 0.9**10
bias_two = 1.0 - 0.95**10
learn_rate = 0.01
decay_rate = 0.1
epsilon = 1e-08


def tenant_of(positions, ends):
    return jnp.sum((positions[:, None] >= ends[None, :]).astype(jnp.int32), axis=1)


def adamw(param, grad, moment, second):
    new_moment = beta_one * moment + (1.0 - beta_one) * grad
    new_second = beta_two * second + (1.0 - beta_two) * grad * grad
    update = new_moment / bias_one / (jnp.sqrt(new_second / bias_two) + epsilon)
    return (param - learn_rate * (update + decay_rate * param), new_moment, new_second)


def partial_grads(
    token_rows, grad_rows, low_a, low_b, positions, rank_rows, token_counts, rank_ends
):
    token_tenant = tenant_of(positions, jnp.cumsum(token_counts))
    row_tenant = tenant_of(rank_rows, rank_ends)
    same_tenant = token_tenant[:, None] == row_tenant[None, :]
    contract = (((1,), (1,)), ((), ()))
    scores_a = lax.dot_general(token_rows, low_a, contract, preferred_element_type=jnp.float32)
    scores_b = lax.dot_general(grad_rows, low_b, contract, preferred_element_type=jnp.float32)
    hidden = jnp.where(same_tenant, scores_a, 0.0).astype(jnp.bfloat16)
    back = jnp.where(same_tenant, scores_b, 0.0).astype(jnp.bfloat16)
    over_tokens = (((0,), (0,)), ((), ()))
    grad_a = lax.dot_general(back, token_rows, over_tokens, preferred_element_type=jnp.float32)
    grad_b = lax.dot_general(hidden, grad_rows, over_tokens, preferred_element_type=jnp.float32)
    return (grad_a, grad_b)


def local_plain(
    tokens,
    cotangent,
    factor_a,
    factor_b,
    moment_a,
    moment_b,
    second_a,
    second_b,
    token_counts,
    rank_blocks,
):
    tok_rows = tokens.shape[0]
    own_rows = moment_a.shape[0]
    context_index = lax.axis_index("ctx")
    replica_index = lax.axis_index("dp")
    rank_ends = jnp.cumsum(rank_blocks * 8)
    half_rows = tok_rows // 2
    token_rows = lax.dynamic_slice_in_dim(tokens, replica_index * half_rows, half_rows, 0)
    grad_rows = lax.dynamic_slice_in_dim(cotangent, replica_index * half_rows, half_rows, 0)
    positions = (
        context_index * tok_rows
        + replica_index * half_rows
        + jnp.arange(half_rows, dtype=jnp.int32)
    )
    all_a, all_b = (
        lax.all_gather(factor_a.astype(jnp.bfloat16), "ctx", axis=0, tiled=True),
        lax.all_gather(factor_b.astype(jnp.bfloat16), "ctx", axis=0, tiled=True),
    )
    rank_rows = jnp.arange(all_a.shape[0], dtype=jnp.int32)
    term_a, term_b = partial_grads(
        token_rows, grad_rows, all_a, all_b, positions, rank_rows, token_counts, rank_ends
    )
    grad_a, grad_b = (
        lax.psum_scatter(term_a, ("ctx", "dp"), scatter_dimension=0, tiled=True),
        lax.psum_scatter(term_b, ("ctx", "dp"), scatter_dimension=0, tiled=True),
    )
    owned_a = lax.dynamic_slice_in_dim(factor_a, replica_index * own_rows, own_rows, 0)
    owned_b = lax.dynamic_slice_in_dim(factor_b, replica_index * own_rows, own_rows, 0)
    step_a, new_moment_a, new_second_a = adamw(owned_a, grad_a, moment_a, second_a)
    step_b, new_moment_b, new_second_b = adamw(owned_b, grad_b, moment_b, second_b)
    new_a, new_b = (
        lax.all_gather(step_a, "dp", axis=0, tiled=True),
        lax.all_gather(step_b, "dp", axis=0, tiled=True),
    )
    return (new_a, new_b, new_moment_a, new_second_a, new_moment_b, new_second_b)


MESH = pl.DeviceIdType.MESH
ANY = pl.BlockSpec(memory_space=pl.ANY)
VMEM = pl.BlockSpec(memory_space=pltpu.VMEM)
HBM = pl.BlockSpec(memory_space=pltpu.HBM)


def ring_kernel(
    n,
    chunks,
    tokens,
    cotangent,
    factor_a,
    factor_b,
    moment_a,
    moment_b,
    second_a,
    second_b,
    token_counts,
    rank_blocks,
    out_a,
    out_b,
    out_moment_a,
    out_second_a,
    out_moment_b,
    out_second_b,
    tok,
    cot,
    param,
    moment,
    second,
    low_a,
    low_b,
    back,
    hidden,
    scores,
    grads,
    whole_in,
    half_in,
    counts,
    blocks,
    load_sem,
    gather_send,
    gather_recv,
    reduce_send,
    reduce_recv,
    pair_send,
    pair_recv,
):
    hops = n // 2
    width_a = factor_a.shape[1]
    width_b = factor_b.shape[1]
    own = moment_a.shape[0]
    toks = tokens.shape[0]
    rows = n * own
    group = lax.axis_index("group")
    ctx = lax.axis_index("ctx")
    core = lax.axis_index("dp")
    column, odd = ctx // 2, ctx % 2
    place = column + odd * (n - 1 - 2 * column)

    def index_at(position):
        q = (position + 2 * n) % n
        return 2 * q + (q // hops) * (2 * n - 1 - 4 * q)

    def block(position):
        return pl.ds(pl.multiple_of(index_at(position) * own, own), own)

    signs = (1, -1)
    neighbours = [(group, index_at(place + s), core) for s in signs]
    partner = (group, ctx, 1 - core)
    my_half = pl.ds(pl.multiple_of(core * own, own), own)
    cols_a, cols_b = pl.ds(0, width_a), pl.ds(width_a, width_b)

    loads = [
        pltpu.make_async_copy(source, target, load_sem.at[i])
        for i, (source, target) in enumerate(
            (
                (factor_b.at[my_half], param.at[:, cols_b]),
                (factor_a.at[my_half], param.at[:, cols_a]),
                (cotangent, cot),
                (tokens, tok),
                (moment_a, moment.at[:, cols_a]),
                (moment_b, moment.at[:, cols_b]),
                (second_a, second.at[:, cols_a]),
                (second_b, second.at[:, cols_b]),
                (token_counts, counts),
                (rank_blocks, blocks),
            )
        )
    ]
    for load in loads:
        load.start()
    barrier = pltpu.get_barrier_semaphore()
    for device in (*neighbours, partner):
        pl.semaphore_signal(barrier, inc=1, device_id=device, device_id_type=MESH)
    mine = block(place)
    loads[0].wait()
    low_b[mine, :] = param[:, width_a:].astype(jnp.bfloat16)
    loads[1].wait()
    low_a[mine, :] = param[:, :width_a].astype(jnp.bfloat16)
    pl.semaphore_wait(barrier, 3)

    sent = []

    quarter = width_a // 2
    pieces = ((low_a, 0, quarter), (low_a, quarter, quarter), (low_b, 0, width_b))
    gathering = {}

    def gather(which, t):
        low, start, width = pieces[which]
        half = width // 2
        for d in range(2):
            if t > 1:
                gathering[which, d].wait_recv()
            if t > hops:
                continue
            where = block(place - signs[d] * (t - 1))
            cols = pl.ds(start + d * half, half) if t == hops else pl.ds(start, width)
            copy = pltpu.make_async_remote_copy(
                src_ref=low.at[where, cols],
                dst_ref=low.at[where, cols],
                send_sem=gather_send.at[which, d, t - 1],
                recv_sem=gather_recv.at[which, d, t - 1],
                device_id=neighbours[d],
                device_id_type=MESH,
            )
            copy.start()
            gathering[which, d] = copy
            sent.append(copy)

    gather(2, 1)
    gather(0, 1)
    gather(2, 2)
    gather(1, 1)
    for t in range(3, hops + 1):
        gather(2, t)
        gather(0, t - 1)
    for t in range(2, hops - 1):
        gather(1, t)

    def tenant(position, counts, scale):
        total = jnp.zeros_like(position)
        end = 0
        for t in range(counts.shape[0]):
            end = end + counts[t] * scale
            total = total + (position >= end).astype(jnp.int32)
        return total

    row = lax.broadcasted_iota(jnp.int32, (rows, 1), 0)
    row = (row // own) * (2 * own) + core * own + row % own
    token = ctx * toks + lax.broadcasted_iota(jnp.int32, (1, toks), 1)
    loads[8].wait()
    loads[9].wait()
    same = tenant(row, blocks, 8) == tenant(token, counts, 1)
    last = (((1,), (1,)), ((), ()))

    gather(2, hops + 1)
    loads[2].wait()
    scores_b = lax.dot_general(low_b[...], cot[...], last, preferred_element_type=jnp.float32)
    back[...] = jnp.where(same, scores_b, 0.0).astype(jnp.bfloat16)
    gather(1, hops - 1)

    reducing = {}

    def reduce_step(c, t):
        start, width = chunks[c]
        half = width // 2
        for d in range(2):
            if t > 1:
                reducing[c, d].wait_recv()
            if t > hops:
                continue
            where = block(place + signs[d] * (hops + 1 - t))
            if t == 1:
                source = grads.at[where, pl.ds(start + d * half, half)]
                target = half_in.at[d, :, pl.ds(start // 2, half)]
            else:
                if t == 2:
                    cols = pl.ds(start + d * half, half)
                    grads[where, cols] += half_in[d, :, start // 2 : start // 2 + half]
                else:
                    cols = pl.ds(start, width)
                    grads[where, cols] += whole_in[d, t - 3, :, start : start + width]
                source = grads.at[where, pl.ds(start, width)]
                target = whole_in.at[d, t - 2, :, pl.ds(start, width)]
            copy = pltpu.make_async_remote_copy(
                src_ref=source,
                dst_ref=target,
                send_sem=reduce_send.at[c, d, t - 1],
                recv_sem=reduce_recv.at[c, d, t - 1],
                device_id=neighbours[d],
                device_id_type=MESH,
            )
            copy.start()
            reducing[c, d] = copy
            sent.append(copy)

    loads[3].wait()
    last_c = len(chunks) - 1
    for c in range(last_c):
        start, width = chunks[c]
        grads[:, start : start + width] = jnp.dot(
            back[...], tok[:, start : start + width], preferred_element_type=jnp.float32
        )
        reduce_step(c, 1)
        if c < 2:
            gather(c, hops)
    def score(start, width, first):
        term = lax.dot_general(
            low_a[:, start : start + width],
            tok[:, start : start + width],
            last,
            preferred_element_type=jnp.float32,
        )
        scores[...] = term if first else scores[...] + term

    later = [(c, t) for t in range(2, hops + 1) for c in range(last_c)]
    for c, (start, width) in enumerate(chunks[:last_c]):
        if c % 2 == 0:
            gather(c // 2, hops + 1)
        score(start, width, c == 0)
        for _ in range(2 if c == 0 else 1):
            reduce_step(*later.pop(0))
    hidden[...] = jnp.where(same, scores[...], 0.0).astype(jnp.bfloat16)
    grads[:, cols_b] = jnp.dot(hidden[...], cot[...], preferred_element_type=jnp.float32)
    t = 1
    while later:
        if t <= hops:
            reduce_step(last_c, t)
            t += 1
        reduce_step(*later.pop(0))

    for load in loads[4:8]:
        load.wait()

    def finish(c):
        start, width = chunks[c]
        cols = pl.ds(start, width)
        reduce_step(c, hops + 1)
        grad = grads[mine, cols] + whole_in[0, hops - 2, :, start : start + width]
        grad = grad + whole_in[1, hops - 2, :, start : start + width]
        new = adamw(param[:, cols], grad, moment[:, cols], second[:, cols])
        if start < width_a:
            outs, at = (out_a, out_moment_a, out_second_a), pl.ds(start, width)
        else:
            outs, at = (out_b, out_moment_b, out_second_b), pl.ds(start - width_a, width)
        outs[0][my_half, at], outs[1][:, at], outs[2][:, at] = new
        copy = pltpu.make_async_remote_copy(
            src_ref=outs[0].at[my_half, at],
            dst_ref=outs[0].at[my_half, at],
            send_sem=pair_send.at[c],
            recv_sem=pair_recv.at[c],
            device_id=partner,
            device_id_type=MESH,
        )
        copy.start()
        sent.append(copy)
        return copy

    pairs = [finish(c) for c in (0, last_c, *range(1, last_c))]
    for pair in pairs:
        pair.wait_recv()
    for copy in sent:
        copy.wait_send()


def hand_out(*refs):
    copies = [
        pltpu.make_async_copy(refs[i], refs[6 + i], refs[12].at[i]) for i in range(6)
    ]
    for copy in copies:
        copy.start()
    for copy in copies:
        copy.wait()


def local_ring(n, *args):
    tokens, cotangent, factor_a, factor_b, moment_a = args[:5]
    toks, width_a = tokens.shape
    width_b = cotangent.shape[1]
    own = moment_a.shape[0]
    width = width_a + width_b
    rows = n * own
    hops = n // 2
    part = width_a // 4
    chunks = (*((i * part, part) for i in range(4)), (width_a, width_b))
    f32, bf16 = jnp.float32, jnp.bfloat16
    count = len(chunks)
    dma = pltpu.SemaphoreType.DMA
    like = jax.ShapeDtypeStruct
    results = pl.pallas_call(
        functools.partial(ring_kernel, n, chunks),
        out_shape=(
            pltpu.VMEM(factor_a.shape, f32),
            pltpu.VMEM(factor_b.shape, f32),
            pltpu.VMEM((own, width_a), f32),
            pltpu.VMEM((own, width_a), f32),
            pltpu.VMEM((own, width_b), f32),
            pltpu.VMEM((own, width_b), f32),
        ),
        in_specs=[HBM] * 10,
        out_specs=(VMEM,) * 6,
        scratch_shapes=[
            pltpu.VMEM((toks, width_a), bf16),
            pltpu.VMEM((toks, width_b), bf16),
            pltpu.VMEM((own, width), f32),
            pltpu.VMEM((own, width), f32),
            pltpu.VMEM((own, width), f32),
            pltpu.VMEM((rows, width_a), bf16),
            pltpu.VMEM((rows, width_b), bf16),
            pltpu.VMEM((rows, toks), bf16),
            pltpu.VMEM((rows, toks), bf16),
            pltpu.VMEM((rows, toks), f32),
            pltpu.VMEM((rows, width), f32),
            pltpu.VMEM((2, hops - 1, own, width), f32),
            pltpu.VMEM((2, own, width // 2), f32),
            pltpu.SMEM(args[8].shape, jnp.int32),
            pltpu.SMEM(args[9].shape, jnp.int32),
            dma((10,)),
            dma((3, 2, hops)),
            dma((3, 2, hops)),
            dma((count, 2, hops)),
            dma((count, 2, hops)),
            dma((count,)),
            dma((count,)),
        ],
        compiler_params=pltpu.CompilerParams(
            collective_id=0, has_side_effects=True, vmem_limit_bytes=50 << 20
        ),
    )(*(pltpu.with_memory_space_constraint(arg, pltpu.HBM) for arg in args))
    return pl.pallas_call(
        hand_out,
        out_shape=tuple(like(r.shape, r.dtype) for r in results),
        in_specs=[VMEM] * 6,
        out_specs=(HBM,) * 6,
        scratch_shapes=[dma((6,))],
        compiler_params=pltpu.CompilerParams(vmem_limit_bytes=4 << 20),
    )(*results)


def solution(mesh):
    n = mesh.shape["ctx"]
    if n >= 4 and n % 2 == 0 and 256 % (32 * n) == 0:
        local = functools.partial(local_ring, n)
    else:
        local = local_plain

    return jax.shard_map(
        local,
        mesh=mesh,
        in_specs=(
            P(("group", "ctx"), None),
            P(("group", "ctx"), None),
            P(("group", "ctx"), None),
            P(("group", "ctx"), None),
            P(("group", "ctx", "dp"), None),
            P(("group", "ctx", "dp"), None),
            P(("group", "ctx", "dp"), None),
            P(("group", "ctx", "dp"), None),
            P("group"),
            P("group"),
        ),
        out_specs=(
            P(("group", "ctx"), None),
            P(("group", "ctx"), None),
            P(("group", "ctx", "dp"), None),
            P(("group", "ctx", "dp"), None),
            P(("group", "ctx", "dp"), None),
            P(("group", "ctx", "dp"), None),
        ),
        check_vma=False,
    )
```

```python
import functools

import jax
import jax.numpy as jnp
from jax import lax
from jax.experimental import pallas as pl
from jax.experimental.pallas import tpu as pltpu
from jax.sharding import PartitionSpec as P

beta_one = 0.9
beta_two = 0.95
bias_one = 1.0 - 0.9**10
bias_two = 1.0 - 0.95**10
learn_rate = 0.01
decay_rate = 0.1
epsilon = 1e-08


def tenant_of(positions, ends):
    return jnp.sum((positions[:, None] >= ends[None, :]).astype(jnp.int32), axis=1)


def adamw(param, grad, moment, second):
    new_moment = beta_one * moment + (1.0 - beta_one) * grad
    new_second = beta_two * second + (1.0 - beta_two) * grad * grad
    update = new_moment / bias_one / (jnp.sqrt(new_second / bias_two) + epsilon)
    return (param - learn_rate * (update + decay_rate * param), new_moment, new_second)


def partial_grads(
    token_rows, grad_rows, low_a, low_b, positions, rank_rows, token_counts, rank_ends
):
    token_tenant = tenant_of(positions, jnp.cumsum(token_counts))
    row_tenant = tenant_of(rank_rows, rank_ends)
    same_tenant = token_tenant[:, None] == row_tenant[None, :]
    contract = (((1,), (1,)), ((), ()))
    scores_a = lax.dot_general(token_rows, low_a, contract, preferred_element_type=jnp.float32)
    scores_b = lax.dot_general(grad_rows, low_b, contract, preferred_element_type=jnp.float32)
    hidden = jnp.where(same_tenant, scores_a, 0.0).astype(jnp.bfloat16)
    back = jnp.where(same_tenant, scores_b, 0.0).astype(jnp.bfloat16)
    over_tokens = (((0,), (0,)), ((), ()))
    grad_a = lax.dot_general(back, token_rows, over_tokens, preferred_element_type=jnp.float32)
    grad_b = lax.dot_general(hidden, grad_rows, over_tokens, preferred_element_type=jnp.float32)
    return (grad_a, grad_b)


def local_plain(
    tokens,
    cotangent,
    factor_a,
    factor_b,
    moment_a,
    moment_b,
    second_a,
    second_b,
    token_counts,
    rank_blocks,
):
    tok_rows = tokens.shape[0]
    own_rows = moment_a.shape[0]
    context_index = lax.axis_index("ctx")
    replica_index = lax.axis_index("dp")
    rank_ends = jnp.cumsum(rank_blocks * 8)
    half_rows = tok_rows // 2
    token_rows = lax.dynamic_slice_in_dim(tokens, replica_index * half_rows, half_rows, 0)
    grad_rows = lax.dynamic_slice_in_dim(cotangent, replica_index * half_rows, half_rows, 0)
    positions = (
        context_index * tok_rows
        + replica_index * half_rows
        + jnp.arange(half_rows, dtype=jnp.int32)
    )
    all_a, all_b = (
        lax.all_gather(factor_a.astype(jnp.bfloat16), "ctx", axis=0, tiled=True),
        lax.all_gather(factor_b.astype(jnp.bfloat16), "ctx", axis=0, tiled=True),
    )
    rank_rows = jnp.arange(all_a.shape[0], dtype=jnp.int32)
    term_a, term_b = partial_grads(
        token_rows, grad_rows, all_a, all_b, positions, rank_rows, token_counts, rank_ends
    )
    grad_a, grad_b = (
        lax.psum_scatter(term_a, ("ctx", "dp"), scatter_dimension=0, tiled=True),
        lax.psum_scatter(term_b, ("ctx", "dp"), scatter_dimension=0, tiled=True),
    )
    owned_a = lax.dynamic_slice_in_dim(factor_a, replica_index * own_rows, own_rows, 0)
    owned_b = lax.dynamic_slice_in_dim(factor_b, replica_index * own_rows, own_rows, 0)
    step_a, new_moment_a, new_second_a = adamw(owned_a, grad_a, moment_a, second_a)
    step_b, new_moment_b, new_second_b = adamw(owned_b, grad_b, moment_b, second_b)
    new_a, new_b = (
        lax.all_gather(step_a, "dp", axis=0, tiled=True),
        lax.all_gather(step_b, "dp", axis=0, tiled=True),
    )
    return (new_a, new_b, new_moment_a, new_second_a, new_moment_b, new_second_b)


MESH = pl.DeviceIdType.MESH
ANY = pl.BlockSpec(memory_space=pl.ANY)
VMEM = pl.BlockSpec(memory_space=pltpu.VMEM)
HBM = pl.BlockSpec(memory_space=pltpu.HBM)


def ring_kernel(
    n,
    chunks,
    tokens,
    cotangent,
    factor_a,
    factor_b,
    moment_a,
    moment_b,
    second_a,
    second_b,
    token_counts,
    rank_blocks,
    out_a,
    out_b,
    out_moment_a,
    out_second_a,
    out_moment_b,
    out_second_b,
    tok,
    cot,
    param,
    moment,
    second,
    low_a,
    low_b,
    back,
    hidden,
    scores,
    grads,
    whole_in,
    half_in,
    counts,
    blocks,
    load_sem,
    gather_send,
    gather_recv,
    reduce_send,
    reduce_recv,
    pair_send,
    pair_recv,
):
    hops = n // 2
    width_a = factor_a.shape[1]
    width_b = factor_b.shape[1]
    own = moment_a.shape[0]
    toks = tokens.shape[0]
    rows = n * own
    group = lax.axis_index("group")
    ctx = lax.axis_index("ctx")
    core = lax.axis_index("dp")
    column, odd = ctx // 2, ctx % 2
    place = column + odd * (n - 1 - 2 * column)

    def index_at(position):
        q = (position + 2 * n) % n
        return 2 * q + (q // hops) * (2 * n - 1 - 4 * q)

    def block(position):
        return pl.ds(pl.multiple_of(index_at(position) * own, own), own)

    signs = (1, -1)
    neighbours = [(group, index_at(place + s), core) for s in signs]
    partner = (group, ctx, 1 - core)
    my_half = pl.ds(pl.multiple_of(core * own, own), own)
    cols_a, cols_b = pl.ds(0, width_a), pl.ds(width_a, width_b)

    loads = [
        pltpu.make_async_copy(source, target, load_sem.at[i])
        for i, (source, target) in enumerate(
            (
                (factor_b.at[my_half], param.at[:, cols_b]),
                (factor_a.at[my_half], param.at[:, cols_a]),
                (cotangent, cot),
                (tokens, tok),
                (moment_a, moment.at[:, cols_a]),
                (moment_b, moment.at[:, cols_b]),
                (second_a, second.at[:, cols_a]),
                (second_b, second.at[:, cols_b]),
                (token_counts, counts),
                (rank_blocks, blocks),
            )
        )
    ]
    for load in loads:
        load.start()
    barrier = pltpu.get_barrier_semaphore()
    for device in (*neighbours, partner):
        pl.semaphore_signal(barrier, inc=1, device_id=device, device_id_type=MESH)
    mine = block(place)
    loads[0].wait()
    low_b[mine, :] = param[:, width_a:].astype(jnp.bfloat16)
    loads[1].wait()
    low_a[mine, :] = param[:, :width_a].astype(jnp.bfloat16)
    pl.semaphore_wait(barrier, 3)

    sent = []

    quarter = width_a // 2
    pieces = ((low_a, 0, quarter), (low_a, quarter, quarter), (low_b, 0, width_b))
    gathering = {}

    def gather(which, t):
        low, start, width = pieces[which]
        half = width // 2
        for d in range(2):
            if t > 1:
                gathering[which, d].wait_recv()
            if t > hops:
                continue
            where = block(place - signs[d] * (t - 1))
            cols = pl.ds(start + d * half, half) if t == hops else pl.ds(start, width)
            copy = pltpu.make_async_remote_copy(
                src_ref=low.at[where, cols],
                dst_ref=low.at[where, cols],
                send_sem=gather_send.at[which, d, t - 1],
                recv_sem=gather_recv.at[which, d, t - 1],
                device_id=neighbours[d],
                device_id_type=MESH,
            )
            copy.start()
            gathering[which, d] = copy
            sent.append(copy)

    gather(2, 1)
    gather(0, 1)
    gather(2, 2)
    gather(1, 1)
    for t in range(3, hops + 1):
        gather(2, t)
        gather(0, t - 1)
    for t in range(2, hops - 1):
        gather(1, t)

    def tenant(position, counts, scale):
        total = jnp.zeros_like(position)
        end = 0
        for t in range(counts.shape[0]):
            end = end + counts[t] * scale
            total = total + (position >= end).astype(jnp.int32)
        return total

    row = lax.broadcasted_iota(jnp.int32, (rows, 1), 0)
    row = (row // own) * (2 * own) + core * own + row % own
    token = ctx * toks + lax.broadcasted_iota(jnp.int32, (1, toks), 1)
    loads[8].wait()
    loads[9].wait()
    same = tenant(row, blocks, 8) == tenant(token, counts, 1)
    last = (((1,), (1,)), ((), ()))

    gather(2, hops + 1)
    loads[2].wait()
    scores_b = lax.dot_general(low_b[...], cot[...], last, preferred_element_type=jnp.float32)
    back[...] = jnp.where(same, scores_b, 0.0).astype(jnp.bfloat16)
    gather(1, hops - 1)

    reducing = {}

    def reduce_step(c, t):
        start, width = chunks[c]
        half = width // 2
        for d in range(2):
            if t > 1:
                reducing[c, d].wait_recv()
            if t > hops:
                continue
            where = block(place + signs[d] * (hops + 1 - t))
            if t == 1:
                source = grads.at[where, pl.ds(start + d * half, half)]
                target = half_in.at[d, :, pl.ds(start // 2, half)]
            else:
                if t == 2:
                    cols = pl.ds(start + d * half, half)
                    grads[where, cols] += half_in[d, :, start // 2 : start // 2 + half]
                else:
                    cols = pl.ds(start, width)
                    grads[where, cols] += whole_in[d, t - 3, :, start : start + width]
                source = grads.at[where, pl.ds(start, width)]
                target = whole_in.at[d, t - 2, :, pl.ds(start, width)]
            copy = pltpu.make_async_remote_copy(
                src_ref=source,
                dst_ref=target,
                send_sem=reduce_send.at[c, d, t - 1],
                recv_sem=reduce_recv.at[c, d, t - 1],
                device_id=neighbours[d],
                device_id_type=MESH,
            )
            copy.start()
            reducing[c, d] = copy
            sent.append(copy)

    loads[3].wait()
    last_c = len(chunks) - 1
    for c in range(last_c):
        start, width = chunks[c]
        grads[:, start : start + width] = jnp.dot(
            back[...], tok[:, start : start + width], preferred_element_type=jnp.float32
        )
        reduce_step(c, 1)
        gather(c, hops)
    def score(start, width, first):
        term = lax.dot_general(
            low_a[:, start : start + width],
            tok[:, start : start + width],
            last,
            preferred_element_type=jnp.float32,
        )
        scores[...] = term if first else scores[...] + term

    later = [(c, t) for t in range(2, hops + 1) for c in range(last_c)]
    for c, (start, width) in enumerate(chunks[:last_c]):
        reduce_step(*later.pop(0))
        gather(c, hops + 1)
        score(start, width, c == 0)
    hidden[...] = jnp.where(same, scores[...], 0.0).astype(jnp.bfloat16)
    grads[:, cols_b] = jnp.dot(hidden[...], cot[...], preferred_element_type=jnp.float32)
    t = 1
    while later or t <= hops:
        if t <= hops:
            reduce_step(last_c, t)
            t += 1
        if later:
            reduce_step(*later.pop(0))

    for load in loads[4:8]:
        load.wait()

    def finish(c):
        start, width = chunks[c]
        cols = pl.ds(start, width)
        reduce_step(c, hops + 1)
        grad = grads[mine, cols] + whole_in[0, hops - 2, :, start : start + width]
        grad = grad + whole_in[1, hops - 2, :, start : start + width]
        new = adamw(param[:, cols], grad, moment[:, cols], second[:, cols])
        if start < width_a:
            outs, at = (out_a, out_moment_a, out_second_a), pl.ds(start, width)
        else:
            outs, at = (out_b, out_moment_b, out_second_b), pl.ds(start - width_a, width)
        outs[0][my_half, at], outs[1][:, at], outs[2][:, at] = new
        copy = pltpu.make_async_remote_copy(
            src_ref=outs[0].at[my_half, at],
            dst_ref=outs[0].at[my_half, at],
            send_sem=pair_send.at[c],
            recv_sem=pair_recv.at[c],
            device_id=partner,
            device_id_type=MESH,
        )
        copy.start()
        sent.append(copy)
        return copy

    pairs = [finish(c) for c in (0, last_c, *range(1, last_c))]
    for pair in pairs:
        pair.wait_recv()
    for copy in sent:
        copy.wait_send()


def hand_out(*refs):
    copies = [
        pltpu.make_async_copy(refs[i], refs[6 + i], refs[12].at[i]) for i in range(6)
    ]
    for copy in copies:
        copy.start()
    for copy in copies:
        copy.wait()


def local_ring(n, *args):
    tokens, cotangent, factor_a, factor_b, moment_a = args[:5]
    toks, width_a = tokens.shape
    width_b = cotangent.shape[1]
    own = moment_a.shape[0]
    width = width_a + width_b
    rows = n * own
    hops = n // 2
    part = width_a // 2
    chunks = (*((i * part, part) for i in range(2)), (width_a, width_b))
    f32, bf16 = jnp.float32, jnp.bfloat16
    count = len(chunks)
    dma = pltpu.SemaphoreType.DMA
    like = jax.ShapeDtypeStruct
    results = pl.pallas_call(
        functools.partial(ring_kernel, n, chunks),
        out_shape=(
            pltpu.VMEM(factor_a.shape, f32),
            pltpu.VMEM(factor_b.shape, f32),
            pltpu.VMEM((own, width_a), f32),
            pltpu.VMEM((own, width_a), f32),
            pltpu.VMEM((own, width_b), f32),
            pltpu.VMEM((own, width_b), f32),
        ),
        in_specs=[HBM] * 10,
        out_specs=(VMEM,) * 6,
        scratch_shapes=[
            pltpu.VMEM((toks, width_a), bf16),
            pltpu.VMEM((toks, width_b), bf16),
            pltpu.VMEM((own, width), f32),
            pltpu.VMEM((own, width), f32),
            pltpu.VMEM((own, width), f32),
            pltpu.VMEM((rows, width_a), bf16),
            pltpu.VMEM((rows, width_b), bf16),
            pltpu.VMEM((rows, toks), bf16),
            pltpu.VMEM((rows, toks), bf16),
            pltpu.VMEM((rows, toks), f32),
            pltpu.VMEM((rows, width), f32),
            pltpu.VMEM((2, hops - 1, own, width), f32),
            pltpu.VMEM((2, own, width // 2), f32),
            pltpu.SMEM(args[8].shape, jnp.int32),
            pltpu.SMEM(args[9].shape, jnp.int32),
            dma((10,)),
            dma((3, 2, hops)),
            dma((3, 2, hops)),
            dma((count, 2, hops)),
            dma((count, 2, hops)),
            dma((count,)),
            dma((count,)),
        ],
        compiler_params=pltpu.CompilerParams(
            collective_id=0, has_side_effects=True, vmem_limit_bytes=50 << 20
        ),
    )(*(pltpu.with_memory_space_constraint(arg, pltpu.HBM) for arg in args))
    return pl.pallas_call(
        hand_out,
        out_shape=tuple(like(r.shape, r.dtype) for r in results),
        in_specs=[VMEM] * 6,
        out_specs=(HBM,) * 6,
        scratch_shapes=[dma((6,))],
        compiler_params=pltpu.CompilerParams(vmem_limit_bytes=4 << 20),
    )(*results)


def solution(mesh):
    n = mesh.shape["ctx"]
    if n >= 4 and n % 2 == 0 and 256 % (32 * n) == 0:
        local = functools.partial(local_ring, n)
    else:
        local = local_plain

    return jax.shard_map(
        local,
        mesh=mesh,
        in_specs=(
            P(("group", "ctx"), None),
            P(("group", "ctx"), None),
            P(("group", "ctx"), None),
            P(("group", "ctx"), None),
            P(("group", "ctx", "dp"), None),
            P(("group", "ctx", "dp"), None),
            P(("group", "ctx", "dp"), None),
            P(("group", "ctx", "dp"), None),
            P("group"),
            P("group"),
        ),
        out_specs=(
            P(("group", "ctx"), None),
            P(("group", "ctx"), None),
            P(("group", "ctx", "dp"), None),
            P(("group", "ctx", "dp"), None),
            P(("group", "ctx", "dp"), None),
            P(("group", "ctx", "dp"), None),
        ),
        check_vma=False,
    )
```
